512 devices in a mesh: seq: 32 (over z, x_hi, core), tok: 16 (over x_lo, y).
Axes of the slice: x: 4 (x_hi: 2, x_lo: 2; x = x_hi * 2 + x_lo), y: 8, z: 8, core: 2. Of those that a mesh axis runs over, the one named last changes fastest.
Arguments:
- cotangent: bfloat16 [32, 2048, 2048], P('seq', 'tok'), may hold values from -6 to 6
- gate_values: bfloat16 [32, 2048, 2048], P('seq', 'tok'), may hold values from -6 to 6
- conv_input: bfloat16 [32, 2048, 2048], P('seq', 'tok'), may hold values from -6 to 6
- filter_taps: float32 [2048, 2048], P('tok', 'seq'), may hold values from -0.125 to 0.125
- first_moment: float32 [2048, 2048], P('tok', 'seq'), may hold values from -12 to 12
- second_moment: float32 [2048, 2048], P('tok', 'seq'), may hold values from 0.1 to 2
Outputs:
- grad_input: bfloat16 [32, 2048, 2048], P('seq', 'tok')
- new_taps: float32 [2048, 2048], P('tok', 'seq')
- new_first: float32 [2048, 2048], P('tok', 'seq')
- new_second: float32 [2048, 2048], P('tok', 'seq')
The draws below stay inside these ranges and needn't reach their ends.
All inputs are finite; a program needn't handle non-finite values.
Results may differ from the reference program's by a relative error of at most 0.0049.
Values may be sent and summed in bfloat16 or wider, within the bound.
A program may use at most 64 MiB of HBM per device.

```python
import math
import jax
import jax.numpy as jnp
from jax import lax

D = 2048
LENGTH = 2048
SEQS = 32


def block_levels(key, extent, pieces, least, largest):
    loudness, own = 1.0, jax.random.fold_in(key, 6)
    for position, blocks in pieces:
        heights = jnp.exp(jax.random.uniform(jax.random.fold_in(own, position), (blocks,), jnp.float32, least / len(pieces), largest / len(pieces)))
        loudness = loudness * jnp.repeat(heights, extent[position] // blocks).reshape([-1 if axis == position else 1 for axis in range(len(extent))])
    return loudness


def centred(stream_key, dims, width, reach, pieces=(), dtype=jnp.bfloat16):
    level = block_levels(stream_key, dims, pieces, -0.22, 0.18) if pieces else 1.0
    values = jax.random.normal(stream_key, dims, jnp.float32) * width * level
    return jnp.minimum(jnp.maximum(values, -reach), reach).astype(dtype)


def setup_inputs(seed: int = 0) -> dict:
    key_of = jax.random.split(jax.random.key(seed), 7)
    return {
        "cotangent": centred(key_of[0], (SEQS, LENGTH, D), 1.0, 6.0, ((0, 32), (1, 16))),
        "gate_values": centred(key_of[1], (SEQS, LENGTH, D), 1.0, 6.0, ((0, 32), (1, 16))),
        "conv_input": centred(key_of[2], (SEQS, LENGTH, D), 1.0, 6.0, ((0, 32), (1, 16))),
        "filter_taps": centred(key_of[3], (D, LENGTH), LENGTH ** -0.5, 0.125, ((0, 16), (1, 32)), jnp.float32),
        "first_moment": centred(key_of[4], (D, LENGTH), 3.0, 12.0, ((0, 16), (1, 32)), jnp.float32),
        "second_moment": jnp.clip(jnp.exp(math.log(2.0) - 2.9957323 * jax.random.uniform(key_of[5], (D, LENGTH), jnp.float32) ** block_levels(key_of[5], (D, LENGTH), ((0, 16), (1, 32)), -0.2, 0.2)), 0.1, 2.0),
    }


beta_one = 0.9
beta_two = 0.999
learn_rate = 0.05
adam_step = 10
adam_eps = 1e-08

def reference(cotangent, gate_values, conv_input, filter_taps, first_moment, second_moment):
    length = conv_input.shape[1]
    total_size = 2 * length
    spec_taps = jnp.fft.rfft(filter_taps.T, n=total_size, axis=0)

    def one_sequence(running, inputs_now):
        tangent, gate_now, source = inputs_now
        spec_source = jnp.fft.rfft(source.astype(jnp.float32), n=total_size, axis=0)
        scaled = lax.optimization_barrier((tangent.astype(jnp.float32) * gate_now.astype(jnp.float32)).astype(jnp.bfloat16)).astype(jnp.float32)
        spec_scaled = jnp.fft.rfft(scaled, n=total_size, axis=0)
        grad_input = jnp.fft.irfft(jnp.conj(spec_taps) * spec_scaled, n=total_size, axis=0)[:length].astype(jnp.bfloat16)
        taps_part = jnp.fft.irfft(jnp.conj(spec_source) * spec_scaled, n=total_size, axis=0)[:length]
        return (running + taps_part, grad_input)
    initial = jnp.zeros((length, filter_taps.shape[0]), jnp.float32)
    summed, grad_input = lax.scan(one_sequence, initial, (cotangent, gate_values, conv_input))
    taps_grad = summed.T / SEQS
    new_first = beta_one * first_moment + (1.0 - beta_one) * taps_grad
    new_second = beta_two * second_moment + (1.0 - beta_two) * taps_grad * taps_grad
    first_hat = new_first / (1.0 - beta_one ** adam_step)
    second_hat = new_second / (1.0 - beta_two ** adam_step)
    new_taps = filter_taps - learn_rate * first_hat / (jnp.sqrt(second_hat) + adam_eps)
    return (grad_input, new_taps, new_first, new_second)
```

```python
import jax
import jax.numpy as jnp
import numpy as np
from jax import lax
from jax.experimental import pallas as pl
from jax.experimental.pallas import tpu as pltpu
from jax.sharding import PartitionSpec as P

beta_one = 0.9
beta_two = 0.999
learn_rate = 0.05
adam_step = 10
adam_eps = 1e-08

MESH = pl.DeviceIdType.MESH
LANES = 128
TOK = 16
OWNERS = 16
LAGS = 64
BLOCK = 256
PAIRS = 4
FREQS = 256


def transform_matrices():
    order = np.concatenate([np.arange(0, FREQS, 2), np.arange(1, FREQS, 2)])
    angle = 2.0 * np.pi * np.outer(order + 0.5, np.arange(BLOCK)) / (2 * BLOCK)
    ahead = np.concatenate([np.cos(angle), -np.sin(angle)])
    back = ahead.T / FREQS

    def split(matrix):
        high = matrix.astype(jnp.bfloat16)
        low = (matrix - high.astype(np.float64)).astype(jnp.bfloat16)
        return np.stack([high, low])

    return split(ahead), split(back)


def forward(source_ref, spec_ref, ahead_ref):
    def pair(p, carry):
        row = pl.multiple_of(p * (2 * BLOCK), 2 * BLOCK)
        both = jnp.concatenate(
            [source_ref[pl.ds(row, BLOCK), :], source_ref[pl.ds(row + BLOCK, BLOCK), :]], axis=1
        )
        spec_ref[p] = jnp.dot(
            ahead_ref[0], both, preferred_element_type=jnp.float32
        ) + jnp.dot(ahead_ref[1], both, preferred_element_type=jnp.float32)
        return carry

    lax.fori_loop(0, PAIRS, pair, 0)


def correlate(left_ref, right_ref, out_ref):
    blocks = 2 * PAIRS

    def tiles(sign, start):
        def tile(step, carry):
            row = pl.multiple_of(start + step * 8, 8)
            real, imag = pl.ds(row, 8), pl.ds(row + FREQS, 8)

            def get(ref, j, rows):
                return ref[j // 2, rows, (j % 2) * LANES : (j % 2 + 1) * LANES]

            left_re = [get(left_ref, j, real) for j in range(blocks)]
            left_im = [get(left_ref, j, imag) for j in range(blocks)]
            right_re = [get(right_ref, j, real) for j in range(blocks)]
            right_im = [get(right_ref, j, imag) for j in range(blocks)]
            win_re, win_im = [right_re[0]], [right_im[0]]
            for d in range(1, blocks):
                if sign > 0:
                    win_re.append(right_re[d] - right_im[d - 1])
                    win_im.append(right_im[d] + right_re[d - 1])
                else:
                    win_re.append(right_re[d] + right_im[d - 1])
                    win_im.append(right_im[d] - right_re[d - 1])
            for i in range(blocks):
                out_re = left_re[i] * win_re[0] + left_im[i] * win_im[0]
                out_im = left_im[i] * win_re[0] - left_re[i] * win_im[0]
                for d in range(1, blocks - i):
                    out_re += left_re[i + d] * win_re[d] + left_im[i + d] * win_im[d]
                    out_im += left_im[i + d] * win_re[d] - left_re[i + d] * win_im[d]
                lanes = slice((i % 2) * LANES, (i % 2 + 1) * LANES)
                out_ref[i // 2, real, lanes] = out_re
                out_ref[i // 2, imag, lanes] = out_im
            return carry

        lax.fori_loop(0, FREQS // 16, tile, 0)

    tiles(1, 0)
    tiles(-1, FREQS // 2)


def backward(spec_ref, back_ref, p):
    both = spec_ref[p].astype(jnp.bfloat16)
    return jnp.dot(back_ref[0], both, preferred_element_type=jnp.float32) + jnp.dot(
        back_ref[1], both, preferred_element_type=jnp.float32
    )


def kernel(
    cot_hbm,
    gate_hbm,
    input_hbm,
    taps_ref,
    ahead_hbm,
    back_hbm,
    grad_out,
    sums_out,
    cot,
    gate,
    ahead,
    back,
    scaled_out,
    input_out,
    scaled_in,
    input_in,
    taps_in,
    grad_buf,
    pair_out,
    pair_in,
    owner_out,
    owner_in,
    spec_scaled,
    spec_right,
    spec_prod,
    sums,
    load_sem,
    input_sem,
    local_sem,
    scaled_send,
    scaled_recv,
    input_send,
    input_recv,
    taps_send,
    taps_recv,
    grad_send,
    grad_recv,
    owner_send,
    owner_recv,
    pair_send,
    pair_recv,
):
    seq, tok = lax.axis_index("seq"), lax.axis_index("tok")
    core, owner = seq % 2, seq // 2
    sibling = (seq + 1 - 2 * core, tok)

    def tok_peer(o):
        return lax.rem(tok + o, TOK)

    def owner_peer(o):
        return lax.rem(owner + o, OWNERS)

    loads = [
        pltpu.make_async_copy(src, dst, load_sem.at[i])
        for i, (src, dst) in enumerate(
            [(cot_hbm.at[0], cot), (gate_hbm.at[0], gate), (ahead_hbm, ahead), (back_hbm, back)]
        )
    ]
    for load in loads:
        load.start()

    def input_load(c):
        lanes = pl.ds(pl.multiple_of(c * LANES, LANES), LANES)
        return pltpu.make_async_copy(
            input_hbm.at[0, :, lanes], input_out.at[c], input_sem.at[c]
        )

    barrier = pltpu.get_barrier_semaphore()

    def greet(o, carry):
        pl.semaphore_signal(barrier, inc=1, device_id=(seq, tok_peer(o)), device_id_type=MESH)
        pl.semaphore_signal(
            barrier, inc=1, device_id=(owner_peer(o) * 2 + core, tok), device_id_type=MESH
        )
        return carry

    lax.fori_loop(1, TOK, greet, 0)
    pl.semaphore_signal(barrier, inc=1, device_id=sibling, device_id_type=MESH)

    def start_input_load(c, carry):
        input_load(c).start()
        return carry

    lax.fori_loop(0, TOK, start_input_load, 0)
    taps_in[owner, core] = jnp.transpose(taps_ref[...]).astype(jnp.bfloat16)
    loads[0].wait()
    loads[1].wait()

    def scale(c, carry):
        lanes = pl.ds(pl.multiple_of(c * LANES, LANES), LANES)
        scaled_out[c] = (
            cot[:, lanes].astype(jnp.float32) * gate[:, lanes].astype(jnp.float32)
        ).astype(jnp.bfloat16)
        return carry

    lax.fori_loop(0, TOK, scale, 0)
    my_rows = pl.ds(pl.multiple_of(tok * LANES, LANES), LANES)
    scaled_in[my_rows, :] = scaled_out[tok]

    def wait_input_load(c, carry):
        input_load(c).wait()
        return carry

    lax.fori_loop(0, TOK, wait_input_load, 0)
    input_in[my_rows, :] = input_out[tok]
    loads[2].wait()
    loads[3].wait()
    pl.semaphore_wait(barrier, 2 * (TOK - 1) + 1)

    def scaled_copy(to, frm):
        rows = pl.ds(pl.multiple_of(frm * LANES, LANES), LANES)
        return pltpu.make_async_remote_copy(
            src_ref=scaled_out.at[to],
            dst_ref=scaled_in.at[rows, :],
            send_sem=scaled_send.at[to],
            recv_sem=scaled_recv.at[frm],
            device_id=(seq, to),
            device_id_type=MESH,
        )

    def input_copy(to, frm):
        rows = pl.ds(pl.multiple_of(frm * LANES, LANES), LANES)
        return pltpu.make_async_remote_copy(
            src_ref=input_out.at[to],
            dst_ref=input_in.at[rows, :],
            send_sem=input_send.at[to],
            recv_sem=input_recv.at[frm],
            device_id=(seq, to),
            device_id_type=MESH,
        )

    def taps_copy(to, frm):
        return pltpu.make_async_remote_copy(
            src_ref=taps_in.at[frm, core],
            dst_ref=taps_in.at[frm, core],
            send_sem=taps_send.at[to],
            recv_sem=taps_recv.at[frm],
            device_id=(to * 2 + core, tok),
            device_id_type=MESH,
        )

    def grad_copy(to, frm):
        return pltpu.make_async_remote_copy(
            src_ref=grad_buf.at[to],
            dst_ref=grad_out.at[frm],
            send_sem=grad_send.at[to],
            recv_sem=grad_recv.at[frm],
            device_id=(seq, to),
            device_id_type=MESH,
        )

    def owner_copy(to, frm):
        return pltpu.make_async_remote_copy(
            src_ref=owner_out.at[to],
            dst_ref=owner_in.at[frm],
            send_sem=owner_send.at[to],
            recv_sem=owner_recv.at[frm],
            device_id=(to * 2 + core, tok),
            device_id_type=MESH,
        )

    def send_first(o, carry):
        scaled_copy(tok_peer(o), tok).start()
        taps_copy(owner_peer(o), owner).start()
        return carry

    lax.fori_loop(1, TOK, send_first, 0)

    def send_input(o, carry):
        input_copy(tok_peer(o), tok).start()
        return carry

    lax.fori_loop(1, TOK, send_input, 0)

    def taps_arrive(o, carry):
        taps_copy(owner, owner_peer(o)).wait_recv()
        return carry

    lax.fori_loop(1, OWNERS, taps_arrive, 0)

    def taps_pair(which):
        return pltpu.make_async_remote_copy(
            src_ref=taps_in.at[:, which],
            dst_ref=taps_in.at[:, which],
            send_sem=pair_send.at[0],
            recv_sem=pair_recv.at[0],
            device_id=sibling,
            device_id_type=MESH,
        )

    taps_pair(core).start()

    def scaled_arrive(o, carry):
        scaled_copy(tok, tok_peer(o)).wait_recv()
        return carry

    lax.fori_loop(1, TOK, scaled_arrive, 0)
    forward(scaled_in, spec_scaled, ahead)
    taps_pair(1 - core).wait_recv()

    def taps_forward(p, carry):
        both = jnp.concatenate(
            [
                taps_in[pl.ds(p * 4, 2)].reshape(BLOCK, LANES),
                taps_in[pl.ds(p * 4 + 2, 2)].reshape(BLOCK, LANES),
            ],
            axis=1,
        )
        spec_right[p] = jnp.dot(
            ahead[0], both, preferred_element_type=jnp.float32
        ) + jnp.dot(ahead[1], both, preferred_element_type=jnp.float32)
        return carry

    lax.fori_loop(0, PAIRS, taps_forward, 0)
    correlate(spec_scaled, spec_right, spec_prod)

    def grad_back(p, carry):
        both = backward(spec_prod, back, p).astype(jnp.bfloat16)
        for half in range(2):
            for part in range(2):
                grad_buf[p * 4 + half * 2 + part] = both[
                    part * LANES : (part + 1) * LANES, half * LANES : (half + 1) * LANES
                ]
        return carry

    lax.fori_loop(0, PAIRS, grad_back, 0)

    def send_grad(o, carry):
        grad_copy(tok_peer(o), tok).start()
        return carry

    lax.fori_loop(1, TOK, send_grad, 0)
    own_grad = pltpu.make_async_copy(grad_buf.at[tok], grad_out.at[tok], local_sem)
    own_grad.start()

    def input_arrive(o, carry):
        input_copy(tok, tok_peer(o)).wait_recv()
        return carry

    lax.fori_loop(1, TOK, input_arrive, 0)
    forward(input_in, spec_right, ahead)
    correlate(spec_scaled, spec_right, spec_prod)

    def sums_back(p, carry):
        both = backward(spec_prod, back, p)
        for half in range(2):
            sums[pl.ds(p * 4 + half * 2, 2)] = both[
                :, half * LANES : (half + 1) * LANES
            ].reshape(2, 2, LAGS, LANES)
        return carry

    lax.fori_loop(0, PAIRS, sums_back, 0)

    def cut(q, carry):
        pair_out[q] = sums[q, 1 - core].astype(jnp.bfloat16)
        return carry

    lax.fori_loop(0, OWNERS, cut, 0)
    pair_copy = pltpu.make_async_remote_copy(
        src_ref=pair_out,
        dst_ref=pair_in,
        send_sem=pair_send.at[1],
        recv_sem=pair_recv.at[1],
        device_id=sibling,
        device_id_type=MESH,
    )
    pair_copy.start()
    pair_copy.wait_recv()

    def join(q, carry):
        owner_out[q] = (sums[q, core] + pair_in[q].astype(jnp.float32)).astype(jnp.bfloat16)
        return carry

    lax.fori_loop(0, OWNERS, join, 0)

    def send_owner(o, carry):
        owner_copy(owner_peer(o), owner).start()
        return carry

    lax.fori_loop(1, OWNERS, send_owner, 0)
    owner_in[owner] = owner_out[owner]

    def owner_arrive(o, carry):
        owner_copy(owner, owner_peer(o)).wait_recv()
        return carry

    lax.fori_loop(1, OWNERS, owner_arrive, 0)
    total = owner_in[0].astype(jnp.float32)
    for q in range(1, OWNERS):
        total += owner_in[q].astype(jnp.float32)
    sums_out[...] = jnp.transpose(total)

    def finish(o, carry):
        scaled_copy(tok_peer(o), tok).wait_send()
        input_copy(tok_peer(o), tok).wait_send()
        taps_copy(owner_peer(o), owner).wait_send()
        grad_copy(tok_peer(o), tok).wait_send()
        owner_copy(owner_peer(o), owner).wait_send()
        grad_copy(tok, tok_peer(o)).wait_recv()
        return carry

    lax.fori_loop(1, TOK, finish, 0)
    taps_pair(core).wait_send()
    pair_copy.wait_send()
    own_grad.wait()


def shards(cotangent, gate_values, conv_input, filter_taps, first_moment, second_moment):
    ahead, back = transform_matrices()
    bf16, f32 = jnp.bfloat16, jnp.float32
    hbm = pl.BlockSpec(memory_space=pl.ANY)
    vmem = pl.BlockSpec(memory_space=pltpu.VMEM)
    width = TOK * LANES
    tokens = 2 * PAIRS * BLOCK
    spec = pltpu.VMEM((PAIRS, 2 * FREQS, 2 * LANES), f32)
    dma = pltpu.SemaphoreType.DMA
    blocks, summed = pl.pallas_call(
        kernel,
        out_shape=(
            jax.ShapeDtypeStruct((TOK, LANES, LANES), bf16),
            jax.ShapeDtypeStruct((LANES, LAGS), f32),
        ),
        in_specs=[hbm, hbm, hbm, vmem, hbm, hbm],
        out_specs=(hbm, vmem),
        scratch_shapes=[
            pltpu.VMEM((LANES, width), bf16),
            pltpu.VMEM((LANES, width), bf16),
            pltpu.VMEM(ahead.shape, bf16),
            pltpu.VMEM(back.shape, bf16),
            pltpu.VMEM((TOK, LANES, LANES), bf16),
            pltpu.VMEM((TOK, LANES, LANES), bf16),
            pltpu.VMEM((tokens, LANES), bf16),
            pltpu.VMEM((tokens, LANES), bf16),
            pltpu.VMEM((OWNERS, 2, LAGS, LANES), bf16),
            pltpu.VMEM((TOK, LANES, LANES), bf16),
            pltpu.VMEM((OWNERS, LAGS, LANES), bf16),
            pltpu.VMEM((OWNERS, LAGS, LANES), bf16),
            pltpu.VMEM((OWNERS, LAGS, LANES), bf16),
            pltpu.VMEM((OWNERS, LAGS, LANES), bf16),
            spec,
            spec,
            spec,
            pltpu.VMEM((OWNERS, 2, LAGS, LANES), f32),
            dma((4,)),
            dma((TOK,)),
            dma,
            dma((TOK,)),
            dma((TOK,)),
            dma((TOK,)),
            dma((TOK,)),
            dma((OWNERS,)),
            dma((OWNERS,)),
            dma((TOK,)),
            dma((TOK,)),
            dma((OWNERS,)),
            dma((OWNERS,)),
            dma((2,)),
            dma((2,)),
        ],
        compiler_params=pltpu.CompilerParams(
            collective_id=0, has_side_effects=True, vmem_limit_bytes=48 << 20
        ),
        name="gated_conv_backward",
    )(cotangent, gate_values, conv_input, filter_taps, ahead, back)
    grad_input = jnp.moveaxis(blocks, 0, 1).reshape(LANES, width)
    taps_grad = summed / lax.axis_size("seq")
    new_first = beta_one * first_moment + (1.0 - beta_one) * taps_grad
    new_second = beta_two * second_moment + (1.0 - beta_two) * taps_grad * taps_grad
    first_hat = new_first / (1.0 - beta_one**adam_step)
    second_hat = new_second / (1.0 - beta_two**adam_step)
    new_taps = filter_taps - learn_rate * first_hat / (jnp.sqrt(second_hat) + adam_eps)
    return (grad_input[None], new_taps, new_first, new_second)


def solution(mesh):
    placed = (
        P("seq", "tok", None),
        P("seq", "tok", None),
        P("seq", "tok", None),
        P("tok", "seq"),
        P("tok", "seq"),
        P("tok", "seq"),
    )
    return jax.shard_map(
        shards,
        mesh=mesh,
        in_specs=placed,
        out_specs=(P("seq", "tok", None), P("tok", "seq"), P("tok", "seq"), P("tok", "seq")),
        check_vma=False,
    )
```

```python
import jax
import jax.numpy as jnp
import numpy as np
from jax import lax
from jax.experimental import pallas as pl
from jax.experimental.pallas import tpu as pltpu
from jax.sharding import PartitionSpec as P

beta_one = 0.9
beta_two = 0.999
learn_rate = 0.05
adam_step = 10
adam_eps = 1e-08

MESH = pl.DeviceIdType.MESH
LANES = 128
TOK = 16
OWNERS = 16
LAGS = 64
BLOCK = 256
PAIRS = 4
PIECES = 16
FREQS = 256


def transform_matrices():
    order = np.concatenate([np.arange(0, FREQS, 2), np.arange(1, FREQS, 2)])
    angle = 2.0 * np.pi * np.outer(order + 0.5, np.arange(BLOCK)) / (2 * BLOCK)
    ahead = np.concatenate([np.cos(angle), -np.sin(angle)])
    back = ahead.T / FREQS

    def split(matrix):
        high = matrix.astype(jnp.bfloat16)
        low = (matrix - high.astype(np.float64)).astype(jnp.bfloat16)
        return np.stack([high, low])

    return split(ahead), split(back)


def forward(source_ref, spec_ref, ahead_ref):
    def pair(p, carry):
        row = pl.multiple_of(p * (2 * BLOCK), 2 * BLOCK)
        both = jnp.concatenate(
            [source_ref[pl.ds(row, BLOCK), :], source_ref[pl.ds(row + BLOCK, BLOCK), :]], axis=1
        )
        spec_ref[p] = jnp.dot(
            ahead_ref[0], both, preferred_element_type=jnp.float32
        ) + jnp.dot(ahead_ref[1], both, preferred_element_type=jnp.float32)
        return carry

    lax.fori_loop(0, PAIRS, pair, 0)


def correlate(left_ref, right_ref, out_ref):
    blocks = 2 * PAIRS

    def tiles(sign, start):
        def tile(step, carry):
            row = pl.multiple_of(start + step * 8, 8)
            real, imag = pl.ds(row, 8), pl.ds(row + FREQS, 8)

            def get(ref, j, rows):
                return ref[j // 2, rows, (j % 2) * LANES : (j % 2 + 1) * LANES]

            left_re = [get(left_ref, j, real) for j in range(blocks)]
            left_im = [get(left_ref, j, imag) for j in range(blocks)]
            right_re = [get(right_ref, j, real) for j in range(blocks)]
            right_im = [get(right_ref, j, imag) for j in range(blocks)]
            win_re, win_im = [right_re[0]], [right_im[0]]
            for d in range(1, blocks):
                if sign > 0:
                    win_re.append(right_re[d] - right_im[d - 1])
                    win_im.append(right_im[d] + right_re[d - 1])
                else:
                    win_re.append(right_re[d] + right_im[d - 1])
                    win_im.append(right_im[d] - right_re[d - 1])
            for i in range(blocks):
                out_re = left_re[i] * win_re[0] + left_im[i] * win_im[0]
                out_im = left_im[i] * win_re[0] - left_re[i] * win_im[0]
                for d in range(1, blocks - i):
                    out_re += left_re[i + d] * win_re[d] + left_im[i + d] * win_im[d]
                    out_im += left_im[i + d] * win_re[d] - left_re[i + d] * win_im[d]
                lanes = slice((i % 2) * LANES, (i % 2 + 1) * LANES)
                out_ref[i // 2, real, lanes] = out_re
                out_ref[i // 2, imag, lanes] = out_im
            return carry

        lax.fori_loop(0, FREQS // 16, tile, 0)

    tiles(1, 0)
    tiles(-1, FREQS // 2)


def backward(spec_ref, back_ref, p):
    both = spec_ref[p].astype(jnp.bfloat16)
    return jnp.dot(back_ref[0], both, preferred_element_type=jnp.float32) + jnp.dot(
        back_ref[1], both, preferred_element_type=jnp.float32
    )


def kernel(
    cot_hbm,
    gate_hbm,
    input_hbm,
    taps_ref,
    ahead_hbm,
    back_hbm,
    grad_out,
    sums_out,
    cot,
    gate,
    ahead,
    back,
    scaled_out,
    input_out,
    scaled_in,
    input_in,
    taps_in,
    grad_buf,
    pair_out,
    pair_in,
    owner_out,
    owner_in,
    spec_scaled,
    spec_right,
    spec_prod,
    sums,
    load_sem,
    input_sem,
    local_sem,
    scaled_send,
    scaled_recv,
    input_send,
    input_recv,
    taps_send,
    taps_recv,
    grad_send,
    grad_recv,
    owner_send,
    owner_recv,
    pair_send,
    pair_recv,
):
    seq, tok = lax.axis_index("seq"), lax.axis_index("tok")
    core, owner = seq % 2, seq // 2
    sibling = (seq + 1 - 2 * core, tok)

    def tok_peer(o):
        return lax.rem(tok + o, TOK)

    def owner_peer(o):
        return lax.rem(owner + o, OWNERS)

    loads = [
        pltpu.make_async_copy(src, dst, load_sem.at[i])
        for i, (src, dst) in enumerate(
            [(cot_hbm.at[0], cot), (gate_hbm.at[0], gate), (ahead_hbm, ahead), (back_hbm, back)]
        )
    ]
    for load in loads:
        load.start()

    def input_load(c):
        lanes = pl.ds(pl.multiple_of(c * LANES, LANES), LANES)
        return pltpu.make_async_copy(
            input_hbm.at[0, :, lanes], input_out.at[c], input_sem.at[c]
        )

    barrier = pltpu.get_barrier_semaphore()

    def greet(o, carry):
        pl.semaphore_signal(barrier, inc=1, device_id=(seq, tok_peer(o)), device_id_type=MESH)
        pl.semaphore_signal(
            barrier, inc=1, device_id=(owner_peer(o) * 2 + core, tok), device_id_type=MESH
        )
        return carry

    lax.fori_loop(1, TOK, greet, 0)
    pl.semaphore_signal(barrier, inc=1, device_id=sibling, device_id_type=MESH)

    def start_input_load(c, carry):
        input_load(c).start()
        return carry

    lax.fori_loop(0, TOK, start_input_load, 0)
    taps_in[owner, core] = taps_ref[...].astype(jnp.bfloat16)
    loads[0].wait()
    loads[1].wait()

    def scale(c, carry):
        lanes = pl.ds(pl.multiple_of(c * LANES, LANES), LANES)
        scaled_out[c] = (
            cot[:, lanes].astype(jnp.float32) * gate[:, lanes].astype(jnp.float32)
        ).astype(jnp.bfloat16)
        return carry

    lax.fori_loop(0, TOK, scale, 0)
    my_rows = pl.ds(pl.multiple_of(tok * LANES, LANES), LANES)
    scaled_in[my_rows, :] = scaled_out[tok]

    def wait_input_load(c, carry):
        input_load(c).wait()
        return carry

    lax.fori_loop(0, TOK, wait_input_load, 0)
    input_in[my_rows, :] = input_out[tok]
    loads[2].wait()
    loads[3].wait()
    pl.semaphore_wait(barrier, 2 * (TOK - 1) + 1)

    def scaled_copy(to, frm):
        rows = pl.ds(pl.multiple_of(frm * LANES, LANES), LANES)
        return pltpu.make_async_remote_copy(
            src_ref=scaled_out.at[to],
            dst_ref=scaled_in.at[rows, :],
            send_sem=scaled_send.at[to],
            recv_sem=scaled_recv.at[frm],
            device_id=(seq, to),
            device_id_type=MESH,
        )

    def input_copy(to, frm):
        rows = pl.ds(pl.multiple_of(frm * LANES, LANES), LANES)
        return pltpu.make_async_remote_copy(
            src_ref=input_out.at[to],
            dst_ref=input_in.at[rows, :],
            send_sem=input_send.at[to],
            recv_sem=input_recv.at[frm],
            device_id=(seq, to),
            device_id_type=MESH,
        )

    def taps_copy(to, frm):
        return pltpu.make_async_remote_copy(
            src_ref=taps_in.at[frm, core],
            dst_ref=taps_in.at[frm, core],
            send_sem=taps_send.at[to],
            recv_sem=taps_recv.at[frm],
            device_id=(to * 2 + core, tok),
            device_id_type=MESH,
        )

    def grad_copy(to, frm):
        lanes = pl.ds(pl.multiple_of(frm * LANES, LANES), LANES)
        return pltpu.make_async_remote_copy(
            src_ref=grad_buf.at[to],
            dst_ref=grad_out.at[0, :, lanes],
            send_sem=grad_send.at[to],
            recv_sem=grad_recv.at[frm],
            device_id=(seq, to),
            device_id_type=MESH,
        )

    def owner_copy(to, frm):
        return pltpu.make_async_remote_copy(
            src_ref=owner_out.at[to],
            dst_ref=owner_in.at[frm],
            send_sem=owner_send.at[to],
            recv_sem=owner_recv.at[frm],
            device_id=(to * 2 + core, tok),
            device_id_type=MESH,
        )

    def send_first(o, carry):
        scaled_copy(tok_peer(o), tok).start()
        taps_copy(owner_peer(o), owner).start()
        return carry

    lax.fori_loop(1, TOK, send_first, 0)

    def send_input(o, carry):
        input_copy(tok_peer(o), tok).start()
        return carry

    lax.fori_loop(1, TOK, send_input, 0)

    def taps_arrive(o, carry):
        taps_copy(owner, owner_peer(o)).wait_recv()
        return carry

    lax.fori_loop(1, OWNERS, taps_arrive, 0)

    def taps_pair(which):
        return pltpu.make_async_remote_copy(
            src_ref=taps_in.at[:, which],
            dst_ref=taps_in.at[:, which],
            send_sem=pair_send.at[0],
            recv_sem=pair_recv.at[0],
            device_id=sibling,
            device_id_type=MESH,
        )

    taps_pair(core).start()

    def scaled_arrive(o, carry):
        scaled_copy(tok, tok_peer(o)).wait_recv()
        return carry

    lax.fori_loop(1, TOK, scaled_arrive, 0)
    forward(scaled_in, spec_scaled, ahead)
    taps_pair(1 - core).wait_recv()

    def taps_forward(p, carry):
        both = jnp.concatenate(
            [
                taps_in[pl.ds(p * 4, 2)].reshape(BLOCK, LANES),
                taps_in[pl.ds(p * 4 + 2, 2)].reshape(BLOCK, LANES),
            ],
            axis=1,
        )
        spec_right[p] = jnp.dot(
            ahead[0], both, preferred_element_type=jnp.float32
        ) + jnp.dot(ahead[1], both, preferred_element_type=jnp.float32)
        return carry

    lax.fori_loop(0, PAIRS, taps_forward, 0)
    correlate(spec_scaled, spec_right, spec_prod)

    def grad_back(p, carry):
        both = backward(spec_prod, back, p).astype(jnp.bfloat16)
        for half in range(2):
            for part in range(2):
                grad_buf[p * 4 + half * 2 + part] = both[
                    part * LANES : (part + 1) * LANES, half * LANES : (half + 1) * LANES
                ]
        return carry

    lax.fori_loop(0, PAIRS, grad_back, 0)

    def send_grad(o, carry):
        grad_copy(tok_peer(o), tok).start()
        return carry

    lax.fori_loop(1, TOK, send_grad, 0)
    my_lanes = pl.ds(pl.multiple_of(tok * LANES, LANES), LANES)
    own_grad = pltpu.make_async_copy(grad_buf.at[tok], grad_out.at[0, :, my_lanes], local_sem)
    own_grad.start()

    def input_arrive(o, carry):
        input_copy(tok, tok_peer(o)).wait_recv()
        return carry

    lax.fori_loop(1, TOK, input_arrive, 0)
    forward(input_in, spec_right, ahead)
    correlate(spec_scaled, spec_right, spec_prod)

    def sums_back(p, carry):
        both = backward(spec_prod, back, p)
        for half in range(2):
            sums[pl.ds(p * 4 + half * 2, 2)] = both[
                :, half * LANES : (half + 1) * LANES
            ].reshape(2, 2, LAGS, LANES)
        return carry

    lax.fori_loop(0, PAIRS, sums_back, 0)

    def cut(q, carry):
        pair_out[q] = sums[q, 1 - core].astype(jnp.bfloat16)
        return carry

    lax.fori_loop(0, OWNERS, cut, 0)
    pair_copy = pltpu.make_async_remote_copy(
        src_ref=pair_out,
        dst_ref=pair_in,
        send_sem=pair_send.at[1],
        recv_sem=pair_recv.at[1],
        device_id=sibling,
        device_id_type=MESH,
    )
    pair_copy.start()
    pair_copy.wait_recv()

    def join(q, carry):
        owner_out[q] = (sums[q, core] + pair_in[q].astype(jnp.float32)).astype(jnp.bfloat16)
        return carry

    lax.fori_loop(0, OWNERS, join, 0)

    def send_owner(o, carry):
        owner_copy(owner_peer(o), owner).start()
        return carry

    lax.fori_loop(1, OWNERS, send_owner, 0)
    owner_in[owner] = owner_out[owner]

    def owner_arrive(o, carry):
        owner_copy(owner, owner_peer(o)).wait_recv()
        return carry

    lax.fori_loop(1, OWNERS, owner_arrive, 0)
    total = owner_in[0].astype(jnp.float32)
    for q in range(1, OWNERS):
        total += owner_in[q].astype(jnp.float32)
    sums_out[...] = total

    def finish(o, carry):
        scaled_copy(tok_peer(o), tok).wait_send()
        input_copy(tok_peer(o), tok).wait_send()
        taps_copy(owner_peer(o), owner).wait_send()
        grad_copy(tok_peer(o), tok).wait_send()
        owner_copy(owner_peer(o), owner).wait_send()
        grad_copy(tok, tok_peer(o)).wait_recv()
        return carry

    lax.fori_loop(1, TOK, finish, 0)
    taps_pair(core).wait_send()
    pair_copy.wait_send()
    own_grad.wait()


def update_kernel(
    grad_ref, sums_ref, taps_ref, first_ref, second_ref, grad_out, taps_out, first_out, second_out, held, in_sem, out_sem
):
    rows = LANES // PIECES
    arrive, leave = [], []
    for i in range(PIECES):
        piece = pl.ds(i * rows, rows)
        arrive.append(pltpu.make_async_copy(grad_ref.at[0, piece], held.at[piece], in_sem.at[i]))
        leave.append(pltpu.make_async_copy(held.at[piece], grad_out.at[0, piece], out_sem.at[i]))
    for copy in arrive:
        copy.start()
    for copy, onward in zip(arrive, leave):
        copy.wait()
        onward.start()
    taps_grad = sums_ref[...] / (2 * OWNERS)
    new_first = beta_one * first_ref[...] + (1.0 - beta_one) * taps_grad
    new_second = beta_two * second_ref[...] + (1.0 - beta_two) * taps_grad * taps_grad
    first_hat = new_first / (1.0 - beta_one**adam_step)
    second_hat = new_second / (1.0 - beta_two**adam_step)
    taps_out[...] = taps_ref[...] - learn_rate * first_hat / (jnp.sqrt(second_hat) + adam_eps)
    first_out[...] = new_first
    second_out[...] = new_second
    for onward in leave:
        onward.wait()


def shards(cotangent, gate_values, conv_input, filter_taps, first_moment, second_moment):
    ahead, back = transform_matrices()
    bf16, f32 = jnp.bfloat16, jnp.float32
    hbm = pl.BlockSpec(memory_space=pl.ANY)
    vmem = pl.BlockSpec(memory_space=pltpu.VMEM)
    width = TOK * LANES
    tokens = 2 * PAIRS * BLOCK
    spec = pltpu.VMEM((PAIRS, 2 * FREQS, 2 * LANES), f32)
    dma = pltpu.SemaphoreType.DMA
    blocks, summed = pl.pallas_call(
        kernel,
        out_shape=(
            jax.ShapeDtypeStruct((1, LANES, width), bf16),
            jax.ShapeDtypeStruct((LAGS, LANES), f32),
        ),
        in_specs=[hbm, hbm, hbm, vmem, hbm, hbm],
        out_specs=(hbm, vmem),
        scratch_shapes=[
            pltpu.VMEM((LANES, width), bf16),
            pltpu.VMEM((LANES, width), bf16),
            pltpu.VMEM(ahead.shape, bf16),
            pltpu.VMEM(back.shape, bf16),
            pltpu.VMEM((TOK, LANES, LANES), bf16),
            pltpu.VMEM((TOK, LANES, LANES), bf16),
            pltpu.VMEM((tokens, LANES), bf16),
            pltpu.VMEM((tokens, LANES), bf16),
            pltpu.VMEM((OWNERS, 2, LAGS, LANES), bf16),
            pltpu.VMEM((TOK, LANES, LANES), bf16),
            pltpu.VMEM((OWNERS, LAGS, LANES), bf16),
            pltpu.VMEM((OWNERS, LAGS, LANES), bf16),
            pltpu.VMEM((OWNERS, LAGS, LANES), bf16),
            pltpu.VMEM((OWNERS, LAGS, LANES), bf16),
            spec,
            spec,
            spec,
            pltpu.VMEM((OWNERS, 2, LAGS, LANES), f32),
            dma((4,)),
            dma((TOK,)),
            dma,
            dma((TOK,)),
            dma((TOK,)),
            dma((TOK,)),
            dma((TOK,)),
            dma((OWNERS,)),
            dma((OWNERS,)),
            dma((TOK,)),
            dma((TOK,)),
            dma((OWNERS,)),
            dma((OWNERS,)),
            dma((2,)),
            dma((2,)),
        ],
        compiler_params=pltpu.CompilerParams(
            collective_id=0, has_side_effects=True, vmem_limit_bytes=60 << 20
        ),
        name="gated_conv_backward",
    )(cotangent, gate_values, conv_input, filter_taps.T, ahead, back)
    piece = jax.ShapeDtypeStruct((LAGS, LANES), f32)
    grad_input, new_taps, new_first, new_second = pl.pallas_call(
        update_kernel,
        out_shape=(jax.ShapeDtypeStruct((1, LANES, width), bf16), piece, piece, piece),
        in_specs=[hbm, vmem, vmem, vmem, vmem],
        out_specs=(hbm, vmem, vmem, vmem),
        scratch_shapes=[pltpu.VMEM((LANES, width), bf16), dma((PIECES,)), dma((PIECES,))],
        name="filter_update",
    )(blocks, summed, filter_taps.T, first_moment.T, second_moment.T)
    return (grad_input, new_taps.T, new_first.T, new_second.T)


def solution(mesh):
    placed = (
        P("seq", "tok", None),
        P("seq", "tok", None),
        P("seq", "tok", None),
        P("tok", "seq"),
        P("tok", "seq"),
        P("tok", "seq"),
    )
    return jax.shard_map(
        shards,
        mesh=mesh,
        in_specs=placed,
        out_specs=(P("seq", "tok", None), P("tok", "seq"), P("tok", "seq"), P("tok", "seq")),
        check_vma=False,
    )
```

```python
import jax
import jax.numpy as jnp
import numpy as np
from jax import lax
from jax.experimental import pallas as pl
from jax.experimental.pallas import tpu as pltpu
from jax.sharding import PartitionSpec as P

beta_one = 0.9
beta_two = 0.999
learn_rate = 0.05
adam_step = 10
adam_eps = 1e-08

MESH = pl.DeviceIdType.MESH
LANES = 128
TOK = 16
DEPTH = 8
OWNERS = 16
PART = 4
LAGS = 64
BLOCK = 256
PAIRS = 4
PIECES = 16
FREQS = 256


def transform_matrices():
    order = np.concatenate([np.arange(0, FREQS, 2), np.arange(1, FREQS, 2)])
    angle = 2.0 * np.pi * np.outer(order + 0.5, np.arange(BLOCK)) / (2 * BLOCK)
    ahead = np.concatenate([np.cos(angle), -np.sin(angle)])
    back = ahead.T / FREQS

    def split(matrix):
        high = matrix.astype(jnp.bfloat16)
        low = (matrix - high.astype(np.float64)).astype(jnp.bfloat16)
        return np.concatenate([high, low], axis=1)

    return split(ahead), split(back)


def spectrum(ahead_ref, both):
    return jnp.dot(
        ahead_ref[...], jnp.concatenate([both, both], axis=0), preferred_element_type=jnp.float32
    )


def forward(source_ref, spec_ref, ahead_ref, first, arrive):
    def pair(step, carry):
        p = lax.rem(first - step + PAIRS, PAIRS)
        arrive(p)
        row = pl.multiple_of(p * (2 * BLOCK), 2 * BLOCK)
        spec_ref[p] = spectrum(
            ahead_ref,
            jnp.concatenate(
                [source_ref[pl.ds(row, BLOCK), :], source_ref[pl.ds(row + BLOCK, BLOCK), :]], axis=1
            ),
        )
        return carry

    lax.fori_loop(0, PAIRS, pair, 0)


def correlate(left_ref, right_ref, out_ref):
    blocks = 2 * PAIRS

    def tiles(sign, start):
        def tile(step, carry):
            row = pl.multiple_of(start + step * 8, 8)
            real, imag = pl.ds(row, 8), pl.ds(row + FREQS, 8)

            def get(ref, j, rows):
                return ref[j // 2, rows, (j % 2) * LANES : (j % 2 + 1) * LANES]

            left_re = [get(left_ref, j, real) for j in range(blocks)]
            left_im = [get(left_ref, j, imag) for j in range(blocks)]
            right_re = [get(right_ref, j, real) for j in range(blocks)]
            right_im = [get(right_ref, j, imag) for j in range(blocks)]
            win_re, win_im = [right_re[0]], [right_im[0]]
            for d in range(1, blocks):
                if sign > 0:
                    win_re.append(right_re[d] - right_im[d - 1])
                    win_im.append(right_im[d] + right_re[d - 1])
                else:
                    win_re.append(right_re[d] + right_im[d - 1])
                    win_im.append(right_im[d] - right_re[d - 1])
            for i in range(blocks):
                out_re = left_re[i] * win_re[0] + left_im[i] * win_im[0]
                out_im = left_im[i] * win_re[0] - left_re[i] * win_im[0]
                for d in range(1, blocks - i):
                    out_re += left_re[i + d] * win_re[d] + left_im[i + d] * win_im[d]
                    out_im += left_im[i + d] * win_re[d] - left_re[i + d] * win_im[d]
                lanes = slice((i % 2) * LANES, (i % 2 + 1) * LANES)
                out_ref[i // 2, real, lanes] = out_re
                out_ref[i // 2, imag, lanes] = out_im
            return carry

        lax.fori_loop(0, FREQS // 16, tile, 0)

    tiles(1, 0)
    tiles(-1, FREQS // 2)


def backward(spec_ref, back_ref, p):
    both = spec_ref[p].astype(jnp.bfloat16)
    return jnp.dot(
        back_ref[...], jnp.concatenate([both, both], axis=0), preferred_element_type=jnp.float32
    )


def kernel(
    cot_hbm,
    gate_hbm,
    input_hbm,
    taps_ref,
    ahead_hbm,
    back_hbm,
    grad_out,
    sums_out,
    cot,
    gate,
    ahead,
    back,
    scaled_out,
    input_out,
    scaled_in,
    input_in,
    taps_in,
    grad_buf,
    pair_out,
    pair_in,
    owner_out,
    owner_in,
    spec_scaled,
    spec_right,
    spec_prod,
    sums,
    load_sem,
    input_sem,
    local_sem,
    scaled_send,
    scaled_recv,
    input_send,
    input_recv,
    taps_send,
    taps_recv,
    grad_send,
    grad_recv,
    owner_send,
    owner_recv,
    pair_send,
    pair_recv,
    hello,
):
    seq, tok = lax.axis_index("seq"), lax.axis_index("tok")
    core, owner = seq % 2, seq // 2
    sibling = (seq + 1 - 2 * core, tok)
    depth, side = owner // 2, owner % 2
    partner = (seq + 2 - 4 * side, tok)
    above, below = (seq + 4, tok), (seq - 4, tok)

    def tok_peer(o):
        return lax.rem(tok + o, TOK)

    def owner_peer(o):
        return lax.rem(owner + o, OWNERS)

    loads = [
        pltpu.make_async_copy(src, dst, load_sem.at[i])
        for i, (src, dst) in enumerate(
            [(cot_hbm.at[0], cot), (gate_hbm.at[0], gate), (ahead_hbm, ahead), (back_hbm, back)]
        )
    ]
    for load in loads:
        load.start()

    def input_load(c):
        lanes = pl.ds(pl.multiple_of(c * LANES, LANES), LANES)
        return pltpu.make_async_copy(
            input_hbm.at[0, :, lanes], input_out.at[c], input_sem.at[c]
        )

    barrier = pltpu.get_barrier_semaphore()

    def greet(o, carry):
        pl.semaphore_signal(barrier, inc=1, device_id=(seq, tok_peer(o)), device_id_type=MESH)
        return carry

    lax.fori_loop(1, TOK, greet, 0)
    pl.semaphore_signal(barrier, inc=1, device_id=sibling, device_id_type=MESH)
    pl.semaphore_signal(barrier, inc=1, device_id=partner, device_id_type=MESH)

    @pl.when(depth > 0)
    def _():
        pl.semaphore_signal(barrier, inc=1, device_id=below, device_id_type=MESH)

    @pl.when(depth < DEPTH - 1)
    def _():
        pl.semaphore_signal(barrier, inc=1, device_id=above, device_id_type=MESH)

    def start_input_load(c, carry):
        input_load(c).start()
        return carry

    lax.fori_loop(0, TOK, start_input_load, 0)
    taps_in[owner, core] = taps_ref[...].astype(jnp.bfloat16)
    loads[0].wait()
    loads[1].wait()

    def scale(c, carry):
        lanes = pl.ds(pl.multiple_of(c * LANES, LANES), LANES)
        scaled_out[c] = (
            cot[:, lanes].astype(jnp.float32) * gate[:, lanes].astype(jnp.float32)
        ).astype(jnp.bfloat16)
        return carry

    lax.fori_loop(0, TOK, scale, 0)
    my_rows = pl.ds(pl.multiple_of(tok * LANES, LANES), LANES)
    scaled_in[my_rows, :] = scaled_out[tok]

    def wait_input_load(c, carry):
        input_load(c).wait()
        return carry

    lax.fori_loop(0, TOK, wait_input_load, 0)
    input_in[my_rows, :] = input_out[tok]
    loads[2].wait()
    loads[3].wait()
    neighbours = jnp.minimum(depth, 1) + jnp.minimum(DEPTH - 1 - depth, 1)
    pl.semaphore_wait(barrier, TOK - 1 + 2 + neighbours)

    def scaled_copy(to, frm):
        rows = pl.ds(pl.multiple_of(frm * LANES, LANES), LANES)
        return pltpu.make_async_remote_copy(
            src_ref=scaled_out.at[to],
            dst_ref=scaled_in.at[rows, :],
            send_sem=scaled_send.at[to],
            recv_sem=scaled_recv.at[frm],
            device_id=(seq, to),
            device_id_type=MESH,
        )

    def input_copy(to, frm):
        rows = pl.ds(pl.multiple_of(frm * LANES, LANES), LANES)
        return pltpu.make_async_remote_copy(
            src_ref=input_out.at[to],
            dst_ref=input_in.at[rows, :],
            send_sem=input_send.at[to],
            recv_sem=input_recv.at[frm],
            device_id=(seq, to),
            device_id_type=MESH,
        )

    def taps_copy(to, frm):
        return pltpu.make_async_remote_copy(
            src_ref=taps_in.at[frm, core],
            dst_ref=taps_in.at[frm, core],
            send_sem=taps_send.at[to],
            recv_sem=taps_recv.at[frm],
            device_id=(to * 2 + core, tok),
            device_id_type=MESH,
        )

    def grad_copy(to, frm):
        lanes = pl.ds(pl.multiple_of(frm * LANES, LANES), LANES)
        return pltpu.make_async_remote_copy(
            src_ref=grad_buf.at[to],
            dst_ref=grad_out.at[0, :, lanes],
            send_sem=grad_send.at[to],
            recv_sem=grad_recv.at[frm],
            device_id=(seq, to),
            device_id_type=MESH,
        )

    def owner_copy(to, frm):
        return pltpu.make_async_remote_copy(
            src_ref=owner_out.at[to],
            dst_ref=owner_in.at[frm],
            send_sem=owner_send.at[to],
            recv_sem=owner_recv.at[frm],
            device_id=(to * 2 + core, tok),
            device_id_type=MESH,
        )

    def send_first(o, carry):
        scaled_copy(tok_peer(o), tok).start()
        peer = owner_peer(o)

        @pl.when(peer // 2 <= depth)
        def _():
            taps_copy(peer, owner).start()

        return carry

    @pl.when(depth > 0)
    def _():
        pl.semaphore_wait(hello.at[0], 1)

    @pl.when(depth < DEPTH - 1)
    def _():
        pl.semaphore_signal(hello.at[0], inc=1, device_id=above, device_id_type=MESH)

    lax.fori_loop(1, TOK, send_first, 0)

    def send_input(o, carry):
        input_copy(tok_peer(o), tok).start()
        return carry

    lax.fori_loop(1, TOK, send_input, 0)

    @pl.when(depth < DEPTH - 1)
    def _():
        pl.semaphore_wait(hello.at[1], 1)

    @pl.when(depth > 0)
    def _():
        pl.semaphore_signal(hello.at[1], inc=1, device_id=below, device_id_type=MESH)

    def send_above(o, carry):
        peer = owner_peer(o)

        @pl.when(peer // 2 > depth)
        def _():
            taps_copy(peer, owner).start()

        return carry

    lax.fori_loop(1, OWNERS, send_above, 0)

    def taps_arrive(o, carry):
        taps_copy(owner, owner_peer(o)).wait_recv()
        return carry

    lax.fori_loop(1, OWNERS, taps_arrive, 0)

    def taps_pair(which):
        return pltpu.make_async_remote_copy(
            src_ref=taps_in.at[:, which],
            dst_ref=taps_in.at[:, which],
            send_sem=pair_send.at[0],
            recv_sem=pair_recv.at[0],
            device_id=sibling,
            device_id_type=MESH,
        )

    taps_pair(core).start()

    def arrivals(copy):
        def arrive(p):
            def one(i, carry):
                peer = p * (TOK // PAIRS) + i

                @pl.when(peer != tok)
                def _():
                    copy(tok, peer).wait_recv()

                return carry

            lax.fori_loop(0, TOK // PAIRS, one, 0)

        return arrive

    earliest = lax.rem(tok // (TOK // PAIRS) + PAIRS - 1, PAIRS)
    forward(scaled_in, spec_scaled, ahead, earliest, arrivals(scaled_copy))
    taps_pair(1 - core).wait_recv()

    def taps_forward(p, carry):
        both = jnp.concatenate(
            [
                taps_in[pl.ds(p * 4, 2)].reshape(BLOCK, LANES),
                taps_in[pl.ds(p * 4 + 2, 2)].reshape(BLOCK, LANES),
            ],
            axis=1,
        )
        spec_right[p] = spectrum(ahead, both)
        return carry

    lax.fori_loop(0, PAIRS, taps_forward, 0)
    correlate(spec_scaled, spec_right, spec_prod)

    def grad_back(p, carry):
        both = backward(spec_prod, back, p).astype(jnp.bfloat16)
        for half in range(2):
            for part in range(2):
                grad_buf[p * 4 + half * 2 + part] = both[
                    part * LANES : (part + 1) * LANES, half * LANES : (half + 1) * LANES
                ]
        return carry

    lax.fori_loop(0, PAIRS, grad_back, 0)

    def send_grad(o, carry):
        grad_copy(tok_peer(o), tok).start()
        return carry

    lax.fori_loop(1, TOK, send_grad, 0)
    my_lanes = pl.ds(pl.multiple_of(tok * LANES, LANES), LANES)
    own_grad = pltpu.make_async_copy(grad_buf.at[tok], grad_out.at[0, :, my_lanes], local_sem)
    own_grad.start()

    forward(input_in, spec_right, ahead, earliest, arrivals(input_copy))
    correlate(spec_scaled, spec_right, spec_prod)

    def pair_copy(p):
        part = pl.ds(p * PART, PART)
        return pltpu.make_async_remote_copy(
            src_ref=pair_out.at[part],
            dst_ref=pair_in.at[part],
            send_sem=pair_send.at[1 + p],
            recv_sem=pair_recv.at[1 + p],
            device_id=sibling,
            device_id_type=MESH,
        )

    def rotated(step):
        return lax.rem(depth // 2 + 1 + step, PAIRS)

    def sums_back(step):
        p = rotated(step)
        both = backward(spec_prod, back, p)
        for half in range(2):
            sums[pl.ds(p * PART + half * 2, 2)] = both[
                :, half * LANES : (half + 1) * LANES
            ].reshape(2, 2, LAGS, LANES)
        for i in range(PART):
            pair_out[p * PART + i] = sums[p * PART + i, 1 - core].astype(jnp.bfloat16)
        pair_copy(p).start()

    def sums_join(step):
        p = rotated(step)
        pair_copy(p).wait_recv()
        for i in range(PART):
            q = p * PART + i
            owner_out[q] = (sums[q, core] + pair_in[q].astype(jnp.float32)).astype(jnp.bfloat16)

            @pl.when(q != owner)
            def _():
                owner_copy(q, owner).start()

    def sums_step(step, carry):
        @pl.when(step < PAIRS)
        def _():
            sums_back(step)

        @pl.when(step > 1)
        def _():
            sums_join(step - 2)

        return carry

    lax.fori_loop(0, PAIRS + 2, sums_step, 0)
    owner_in[owner] = owner_out[owner]

    def owner_arrive(o, carry):
        owner_copy(owner, owner_peer(o)).wait_recv()
        return carry

    lax.fori_loop(1, OWNERS, owner_arrive, 0)
    total = owner_in[0].astype(jnp.float32)
    for q in range(1, OWNERS):
        total += owner_in[q].astype(jnp.float32)
    sums_out[...] = total

    def finish(o, carry):
        scaled_copy(tok_peer(o), tok).wait_send()
        input_copy(tok_peer(o), tok).wait_send()
        taps_copy(owner_peer(o), owner).wait_send()
        grad_copy(tok_peer(o), tok).wait_send()
        owner_copy(owner_peer(o), owner).wait_send()
        grad_copy(tok, tok_peer(o)).wait_recv()
        return carry

    lax.fori_loop(1, TOK, finish, 0)
    taps_pair(core).wait_send()

    def paired(p, carry):
        pair_copy(p).wait_send()
        return carry

    lax.fori_loop(0, PAIRS, paired, 0)
    own_grad.wait()


def update_kernel(
    grad_ref, sums_ref, taps_ref, first_ref, second_ref, grad_out, taps_out, first_out, second_out, held, in_sem, out_sem
):
    rows = LANES // PIECES
    arrive, leave = [], []
    for i in range(PIECES):
        piece = pl.ds(i * rows, rows)
        arrive.append(pltpu.make_async_copy(grad_ref.at[0, piece], held.at[piece], in_sem.at[i]))
        leave.append(pltpu.make_async_copy(held.at[piece], grad_out.at[0, piece], out_sem.at[i]))
    for copy in arrive:
        copy.start()
    for copy, onward in zip(arrive, leave):
        copy.wait()
        onward.start()
    taps_grad = sums_ref[...] / (2 * OWNERS)
    new_first = beta_one * first_ref[...] + (1.0 - beta_one) * taps_grad
    new_second = beta_two * second_ref[...] + (1.0 - beta_two) * taps_grad * taps_grad
    first_hat = new_first / (1.0 - beta_one**adam_step)
    second_hat = new_second / (1.0 - beta_two**adam_step)
    taps_out[...] = taps_ref[...] - learn_rate * first_hat / (jnp.sqrt(second_hat) + adam_eps)
    first_out[...] = new_first
    second_out[...] = new_second
    for onward in leave:
        onward.wait()


def shards(cotangent, gate_values, conv_input, filter_taps, first_moment, second_moment):
    ahead, back = transform_matrices()
    bf16, f32 = jnp.bfloat16, jnp.float32
    hbm = pl.BlockSpec(memory_space=pl.ANY)
    vmem = pl.BlockSpec(memory_space=pltpu.VMEM)
    width = TOK * LANES
    tokens = 2 * PAIRS * BLOCK
    spec = pltpu.VMEM((PAIRS, 2 * FREQS, 2 * LANES), f32)
    dma = pltpu.SemaphoreType.DMA
    blocks, summed = pl.pallas_call(
        kernel,
        out_shape=(
            jax.ShapeDtypeStruct((1, LANES, width), bf16),
            jax.ShapeDtypeStruct((LAGS, LANES), f32),
        ),
        in_specs=[hbm, hbm, hbm, vmem, hbm, hbm],
        out_specs=(hbm, vmem),
        scratch_shapes=[
            pltpu.VMEM((LANES, width), bf16),
            pltpu.VMEM((LANES, width), bf16),
            pltpu.VMEM(ahead.shape, bf16),
            pltpu.VMEM(back.shape, bf16),
            pltpu.VMEM((TOK, LANES, LANES), bf16),
            pltpu.VMEM((TOK, LANES, LANES), bf16),
            pltpu.VMEM((tokens, LANES), bf16),
            pltpu.VMEM((tokens, LANES), bf16),
            pltpu.VMEM((OWNERS, 2, LAGS, LANES), bf16),
            pltpu.VMEM((TOK, LANES, LANES), bf16),
            pltpu.VMEM((OWNERS, LAGS, LANES), bf16),
            pltpu.VMEM((OWNERS, LAGS, LANES), bf16),
            pltpu.VMEM((OWNERS, LAGS, LANES), bf16),
            pltpu.VMEM((OWNERS, LAGS, LANES), bf16),
            spec,
            spec,
            spec,
            pltpu.VMEM((OWNERS, 2, LAGS, LANES), f32),
            dma((4,)),
            dma((TOK,)),
            dma,
            dma((TOK,)),
            dma((TOK,)),
            dma((TOK,)),
            dma((TOK,)),
            dma((OWNERS,)),
            dma((OWNERS,)),
            dma((TOK,)),
            dma((TOK,)),
            dma((OWNERS,)),
            dma((OWNERS,)),
            dma((1 + PAIRS,)),
            dma((1 + PAIRS,)),
            pltpu.SemaphoreType.REGULAR((2,)),
        ],
        compiler_params=pltpu.CompilerParams(
            collective_id=0, has_side_effects=True, vmem_limit_bytes=60 << 20
        ),
        name="gated_conv_backward",
    )(cotangent, gate_values, conv_input, filter_taps.T, ahead, back)
    piece = jax.ShapeDtypeStruct((LAGS, LANES), f32)
    grad_input, new_taps, new_first, new_second = pl.pallas_call(
        update_kernel,
        out_shape=(jax.ShapeDtypeStruct((1, LANES, width), bf16), piece, piece, piece),
        in_specs=[hbm, vmem, vmem, vmem, vmem],
        out_specs=(hbm, vmem, vmem, vmem),
        scratch_shapes=[pltpu.VMEM((LANES, width), bf16), dma((PIECES,)), dma((PIECES,))],
        name="filter_update",
    )(blocks, summed, filter_taps.T, first_moment.T, second_moment.T)
    return (grad_input, new_taps.T, new_first.T, new_second.T)


def solution(mesh):
    placed = (
        P("seq", "tok", None),
        P("seq", "tok", None),
        P("seq", "tok", None),
        P("tok", "seq"),
        P("tok", "seq"),
        P("tok", "seq"),
    )
    return jax.shard_map(
        shards,
        mesh=mesh,
        in_specs=placed,
        out_specs=(P("seq", "tok", None), P("tok", "seq"), P("tok", "seq"), P("tok", "seq")),
        check_vma=False,
    )
```

```python
import jax
import jax.numpy as jnp
import numpy as np
from jax import lax
from jax.experimental import pallas as pl
from jax.experimental.pallas import tpu as pltpu
from jax.sharding import PartitionSpec as P

beta_one = 0.9
beta_two = 0.999
learn_rate = 0.05
adam_step = 10
adam_eps = 1e-08

MESH = pl.DeviceIdType.MESH
LANES = 128
TOK = 16
DEPTH = 8
OWNERS = 16
PART = 4
LAGS = 64
BLOCK = 256
PAIRS = 4
PIECES = 16
FREQS = 256


def transform_matrices():
    order = np.concatenate([np.arange(0, FREQS, 2), np.arange(1, FREQS, 2)])
    angle = 2.0 * np.pi * np.outer(order + 0.5, np.arange(BLOCK)) / (2 * BLOCK)
    ahead = np.concatenate([np.cos(angle), -np.sin(angle)])
    back = ahead.T / FREQS

    def split(matrix):
        high = matrix.astype(jnp.bfloat16)
        low = (matrix - high.astype(np.float64)).astype(jnp.bfloat16)
        return np.concatenate([high, low], axis=1)

    return split(ahead), split(back)


def spectrum(ahead_ref, both):
    return jnp.dot(
        ahead_ref[...], jnp.concatenate([both, both], axis=0), preferred_element_type=jnp.float32
    )


def forward(source_ref, spec_ref, ahead_ref, first, arrive):
    def pair(step, carry):
        p = lax.rem(first - step + PAIRS, PAIRS)
        arrive(p)
        row = pl.multiple_of(p * (2 * BLOCK), 2 * BLOCK)
        spec_ref[p] = spectrum(
            ahead_ref,
            jnp.concatenate(
                [source_ref[pl.ds(row, BLOCK), :], source_ref[pl.ds(row + BLOCK, BLOCK), :]], axis=1
            ),
        )
        return carry

    lax.fori_loop(0, PAIRS, pair, 0)


def correlate(left_ref, right_ref, out_ref):
    blocks = 2 * PAIRS

    def tiles(sign, start):
        def tile(step, carry):
            row = pl.multiple_of(start + step * 8, 8)
            real, imag = pl.ds(row, 8), pl.ds(row + FREQS, 8)

            def get(ref, j, rows):
                return ref[j // 2, rows, (j % 2) * LANES : (j % 2 + 1) * LANES]

            left_re = [get(left_ref, j, real) for j in range(blocks)]
            left_im = [get(left_ref, j, imag) for j in range(blocks)]
            right_re = [get(right_ref, j, real) for j in range(blocks)]
            right_im = [get(right_ref, j, imag) for j in range(blocks)]
            win_re, win_im = [right_re[0]], [right_im[0]]
            for d in range(1, blocks):
                if sign > 0:
                    win_re.append(right_re[d] - right_im[d - 1])
                    win_im.append(right_im[d] + right_re[d - 1])
                else:
                    win_re.append(right_re[d] + right_im[d - 1])
                    win_im.append(right_im[d] - right_re[d - 1])
            for i in range(blocks):
                out_re = left_re[i] * win_re[0] + left_im[i] * win_im[0]
                out_im = left_im[i] * win_re[0] - left_re[i] * win_im[0]
                for d in range(1, blocks - i):
                    out_re += left_re[i + d] * win_re[d] + left_im[i + d] * win_im[d]
                    out_im += left_im[i + d] * win_re[d] - left_re[i + d] * win_im[d]
                lanes = slice((i % 2) * LANES, (i % 2 + 1) * LANES)
                out_ref[i // 2, real, lanes] = out_re
                out_ref[i // 2, imag, lanes] = out_im
            return carry

        lax.fori_loop(0, FREQS // 16, tile, 0)

    tiles(1, 0)
    tiles(-1, FREQS // 2)


def backward(spec_ref, back_ref, p):
    both = spec_ref[p].astype(jnp.bfloat16)
    return jnp.dot(
        back_ref[...], jnp.concatenate([both, both], axis=0), preferred_element_type=jnp.float32
    )


def kernel(
    cot_hbm,
    gate_hbm,
    input_hbm,
    taps_ref,
    ahead_hbm,
    back_hbm,
    grad_out,
    sums_out,
    cot,
    gate,
    ahead,
    back,
    scaled_out,
    input_out,
    scaled_in,
    input_in,
    taps_in,
    grad_buf,
    pair_out,
    pair_in,
    owner_out,
    owner_in,
    spec_scaled,
    spec_right,
    spec_prod,
    sums,
    load_sem,
    input_sem,
    local_sem,
    scaled_send,
    scaled_recv,
    input_send,
    input_recv,
    taps_send,
    taps_recv,
    grad_send,
    grad_recv,
    owner_send,
    owner_recv,
    pair_send,
    pair_recv,
    hello,
):
    seq, tok = lax.axis_index("seq"), lax.axis_index("tok")
    core, owner = seq % 2, seq // 2
    sibling = (seq + 1 - 2 * core, tok)
    depth, side = owner // 2, owner % 2
    partner = (seq + 2 - 4 * side, tok)
    above, below = (seq + 4, tok), (seq - 4, tok)

    def tok_peer(o):
        return lax.rem(tok + o, TOK)

    def owner_peer(o):
        return lax.rem(owner + o, OWNERS)

    loads = [
        pltpu.make_async_copy(src, dst, load_sem.at[i])
        for i, (src, dst) in enumerate(
            [(cot_hbm.at[0], cot), (gate_hbm.at[0], gate), (ahead_hbm, ahead), (back_hbm, back)]
        )
    ]
    for load in loads:
        load.start()

    def input_load(c):
        lanes = pl.ds(pl.multiple_of(c * LANES, LANES), LANES)
        return pltpu.make_async_copy(
            input_hbm.at[0, :, lanes], input_out.at[c], input_sem.at[c]
        )

    barrier = pltpu.get_barrier_semaphore()

    def greet(o, carry):
        pl.semaphore_signal(barrier, inc=1, device_id=(seq, tok_peer(o)), device_id_type=MESH)
        return carry

    lax.fori_loop(1, TOK, greet, 0)
    pl.semaphore_signal(barrier, inc=1, device_id=sibling, device_id_type=MESH)
    pl.semaphore_signal(barrier, inc=1, device_id=partner, device_id_type=MESH)

    @pl.when(depth > 0)
    def _():
        pl.semaphore_signal(barrier, inc=1, device_id=below, device_id_type=MESH)

    @pl.when(depth < DEPTH - 1)
    def _():
        pl.semaphore_signal(barrier, inc=1, device_id=above, device_id_type=MESH)

    def start_input_load(c, carry):
        input_load(c).start()
        return carry

    lax.fori_loop(0, TOK, start_input_load, 0)
    taps_in[owner, core] = taps_ref[...].astype(jnp.bfloat16)
    loads[0].wait()
    loads[1].wait()

    def scale(c, carry):
        lanes = pl.ds(pl.multiple_of(c * LANES, LANES), LANES)
        scaled_out[c] = (
            cot[:, lanes].astype(jnp.float32) * gate[:, lanes].astype(jnp.float32)
        ).astype(jnp.bfloat16)
        return carry

    lax.fori_loop(0, TOK, scale, 0)
    my_rows = pl.ds(pl.multiple_of(tok * LANES, LANES), LANES)
    scaled_in[my_rows, :] = scaled_out[tok]

    def wait_input_load(c, carry):
        input_load(c).wait()
        return carry

    lax.fori_loop(0, TOK, wait_input_load, 0)
    input_in[my_rows, :] = input_out[tok]
    loads[2].wait()
    loads[3].wait()
    neighbours = jnp.minimum(depth, 1) + jnp.minimum(DEPTH - 1 - depth, 1)
    pl.semaphore_wait(barrier, TOK - 1 + 2 + neighbours)

    def scaled_copy(to, frm):
        rows = pl.ds(pl.multiple_of(frm * LANES, LANES), LANES)
        return pltpu.make_async_remote_copy(
            src_ref=scaled_out.at[to],
            dst_ref=scaled_in.at[rows, :],
            send_sem=scaled_send.at[to],
            recv_sem=scaled_recv.at[frm],
            device_id=(seq, to),
            device_id_type=MESH,
        )

    def input_copy(to, frm):
        rows = pl.ds(pl.multiple_of(frm * LANES, LANES), LANES)
        return pltpu.make_async_remote_copy(
            src_ref=input_out.at[to],
            dst_ref=input_in.at[rows, :],
            send_sem=input_send.at[to],
            recv_sem=input_recv.at[frm],
            device_id=(seq, to),
            device_id_type=MESH,
        )

    def taps_copy(to, frm):
        return pltpu.make_async_remote_copy(
            src_ref=taps_in.at[frm, core],
            dst_ref=taps_in.at[frm, core],
            send_sem=taps_send.at[to],
            recv_sem=taps_recv.at[frm],
            device_id=(to * 2 + core, tok),
            device_id_type=MESH,
        )

    def grad_copy(to, frm):
        lanes = pl.ds(pl.multiple_of(frm * LANES, LANES), LANES)
        return pltpu.make_async_remote_copy(
            src_ref=grad_buf.at[to],
            dst_ref=grad_out.at[0, :, lanes],
            send_sem=grad_send.at[to],
            recv_sem=grad_recv.at[frm],
            device_id=(seq, to),
            device_id_type=MESH,
        )

    def owner_copy(to, frm):
        return pltpu.make_async_remote_copy(
            src_ref=owner_out.at[to],
            dst_ref=owner_in.at[frm],
            send_sem=owner_send.at[to],
            recv_sem=owner_recv.at[frm],
            device_id=(to * 2 + core, tok),
            device_id_type=MESH,
        )

    def send_first(o, carry):
        scaled_copy(tok_peer(o), tok).start()
        peer = owner_peer(o)

        @pl.when(peer // 2 <= depth)
        def _():
            taps_copy(peer, owner).start()

        return carry

    @pl.when(depth > 0)
    def _():
        pl.semaphore_wait(hello.at[0], 1)

    @pl.when(depth < DEPTH - 1)
    def _():
        pl.semaphore_signal(hello.at[0], inc=1, device_id=above, device_id_type=MESH)

    lax.fori_loop(1, TOK, send_first, 0)

    def send_input(o, carry):
        input_copy(tok_peer(o), tok).start()
        return carry


    @pl.when(depth < DEPTH - 1)
    def _():
        pl.semaphore_wait(hello.at[1], 1)

    @pl.when(depth > 0)
    def _():
        pl.semaphore_signal(hello.at[1], inc=1, device_id=below, device_id_type=MESH)

    def send_above(o, carry):
        peer = owner_peer(o)

        @pl.when(peer // 2 > depth)
        def _():
            taps_copy(peer, owner).start()

        return carry

    lax.fori_loop(1, OWNERS, send_above, 0)
    lax.fori_loop(1, TOK, send_input, 0)

    def taps_arrive(o, carry):
        taps_copy(owner, owner_peer(o)).wait_recv()
        return carry

    lax.fori_loop(1, OWNERS, taps_arrive, 0)

    def taps_pair(which):
        return pltpu.make_async_remote_copy(
            src_ref=taps_in.at[:, which],
            dst_ref=taps_in.at[:, which],
            send_sem=pair_send.at[0],
            recv_sem=pair_recv.at[0],
            device_id=sibling,
            device_id_type=MESH,
        )

    taps_pair(core).start()

    def arrivals(copy):
        def arrive(p):
            def one(i, carry):
                peer = p * (TOK // PAIRS) + i

                @pl.when(peer != tok)
                def _():
                    copy(tok, peer).wait_recv()

                return carry

            lax.fori_loop(0, TOK // PAIRS, one, 0)

        return arrive

    earliest = lax.rem(tok // (TOK // PAIRS) + PAIRS - 1, PAIRS)
    forward(scaled_in, spec_scaled, ahead, earliest, arrivals(scaled_copy))
    taps_pair(1 - core).wait_recv()

    def taps_forward(p, carry):
        both = jnp.concatenate(
            [
                taps_in[pl.ds(p * 4, 2)].reshape(BLOCK, LANES),
                taps_in[pl.ds(p * 4 + 2, 2)].reshape(BLOCK, LANES),
            ],
            axis=1,
        )
        spec_right[p] = spectrum(ahead, both)
        return carry

    lax.fori_loop(0, PAIRS, taps_forward, 0)
    correlate(spec_scaled, spec_right, spec_prod)

    def grad_back(p, carry):
        both = backward(spec_prod, back, p).astype(jnp.bfloat16)
        for half in range(2):
            for part in range(2):
                grad_buf[p * 4 + half * 2 + part] = both[
                    part * LANES : (part + 1) * LANES, half * LANES : (half + 1) * LANES
                ]
        return carry

    lax.fori_loop(0, PAIRS, grad_back, 0)

    def send_grad(o, carry):
        grad_copy(tok_peer(o), tok).start()
        return carry

    lax.fori_loop(1, TOK, send_grad, 0)
    my_lanes = pl.ds(pl.multiple_of(tok * LANES, LANES), LANES)
    own_grad = pltpu.make_async_copy(grad_buf.at[tok], grad_out.at[0, :, my_lanes], local_sem)
    own_grad.start()

    forward(input_in, spec_right, ahead, earliest, arrivals(input_copy))
    correlate(spec_scaled, spec_right, spec_prod)

    def pair_copy(p):
        part = pl.ds(p * PART, PART)
        return pltpu.make_async_remote_copy(
            src_ref=pair_out.at[part],
            dst_ref=pair_in.at[part],
            send_sem=pair_send.at[1 + p],
            recv_sem=pair_recv.at[1 + p],
            device_id=sibling,
            device_id_type=MESH,
        )

    def rotated(step):
        return lax.rem(depth // 2 + 1 + step, PAIRS)

    def sums_back(step):
        p = rotated(step)
        both = backward(spec_prod, back, p)
        for half in range(2):
            sums[pl.ds(p * PART + half * 2, 2)] = both[
                :, half * LANES : (half + 1) * LANES
            ].reshape(2, 2, LAGS, LANES)
        for i in range(PART):
            pair_out[p * PART + i] = sums[p * PART + i, 1 - core].astype(jnp.bfloat16)
        pair_copy(p).start()

    def sums_join(step):
        p = rotated(step)
        pair_copy(p).wait_recv()
        for i in range(PART):
            q = p * PART + i
            owner_out[q] = (sums[q, core] + pair_in[q].astype(jnp.float32)).astype(jnp.bfloat16)

            @pl.when(q != owner)
            def _():
                owner_copy(q, owner).start()

    def sums_step(step, carry):
        @pl.when(step < PAIRS)
        def _():
            sums_back(step)

        @pl.when(step > 1)
        def _():
            sums_join(step - 2)

        return carry

    lax.fori_loop(0, PAIRS + 2, sums_step, 0)
    owner_in[owner] = owner_out[owner]

    def owner_arrive(o, carry):
        owner_copy(owner, owner_peer(o)).wait_recv()
        return carry

    lax.fori_loop(1, OWNERS, owner_arrive, 0)
    total = owner_in[0].astype(jnp.float32)
    for q in range(1, OWNERS):
        total += owner_in[q].astype(jnp.float32)
    sums_out[...] = total

    def finish(o, carry):
        scaled_copy(tok_peer(o), tok).wait_send()
        input_copy(tok_peer(o), tok).wait_send()
        taps_copy(owner_peer(o), owner).wait_send()
        grad_copy(tok_peer(o), tok).wait_send()
        owner_copy(owner_peer(o), owner).wait_send()
        grad_copy(tok, tok_peer(o)).wait_recv()
        return carry

    lax.fori_loop(1, TOK, finish, 0)
    taps_pair(core).wait_send()

    def paired(p, carry):
        pair_copy(p).wait_send()
        return carry

    lax.fori_loop(0, PAIRS, paired, 0)
    own_grad.wait()


def update_kernel(
    grad_ref, sums_ref, taps_ref, first_ref, second_ref,
    grad_out, taps_out, first_out, second_out,
    held, small, done, in_sem, out_sem, small_sem, done_sem,
):
    rows = LANES // PIECES
    smalls = [
        pltpu.make_async_copy(ref, small.at[i], small_sem.at[i])
        for i, ref in enumerate((sums_ref, taps_ref, first_ref, second_ref))
    ]
    arrive, leave = [], []
    for i in range(PIECES):
        piece = pl.ds(i * rows, rows)
        arrive.append(pltpu.make_async_copy(grad_ref.at[0, piece], held.at[piece], in_sem.at[i]))
        leave.append(pltpu.make_async_copy(held.at[piece], grad_out.at[0, piece], out_sem.at[i]))
    for copy in smalls + arrive:
        copy.start()
    for copy in smalls:
        copy.wait()
    taps_grad = small[0] / (2 * OWNERS)
    new_first = beta_one * small[2] + (1.0 - beta_one) * taps_grad
    new_second = beta_two * small[3] + (1.0 - beta_two) * taps_grad * taps_grad
    first_hat = new_first / (1.0 - beta_one**adam_step)
    second_hat = new_second / (1.0 - beta_two**adam_step)
    done[0] = small[1] - learn_rate * first_hat / (jnp.sqrt(second_hat) + adam_eps)
    done[1] = new_first
    done[2] = new_second
    finished = [
        pltpu.make_async_copy(done.at[i], ref, done_sem.at[i])
        for i, ref in enumerate((taps_out, first_out, second_out))
    ]
    for copy in finished:
        copy.start()
    for copy, onward in zip(arrive, leave):
        copy.wait()
        onward.start()
    for copy in finished + leave:
        copy.wait()


def shards(cotangent, gate_values, conv_input, filter_taps, first_moment, second_moment):
    ahead, back = transform_matrices()
    bf16, f32 = jnp.bfloat16, jnp.float32
    hbm = pl.BlockSpec(memory_space=pl.ANY)
    vmem = pl.BlockSpec(memory_space=pltpu.VMEM)
    width = TOK * LANES
    tokens = 2 * PAIRS * BLOCK
    spec = pltpu.VMEM((PAIRS, 2 * FREQS, 2 * LANES), f32)
    dma = pltpu.SemaphoreType.DMA
    blocks, summed = pl.pallas_call(
        kernel,
        out_shape=(
            jax.ShapeDtypeStruct((1, LANES, width), bf16),
            jax.ShapeDtypeStruct((LAGS, LANES), f32),
        ),
        in_specs=[hbm, hbm, hbm, vmem, hbm, hbm],
        out_specs=(hbm, vmem),
        scratch_shapes=[
            pltpu.VMEM((LANES, width), bf16),
            pltpu.VMEM((LANES, width), bf16),
            pltpu.VMEM(ahead.shape, bf16),
            pltpu.VMEM(back.shape, bf16),
            pltpu.VMEM((TOK, LANES, LANES), bf16),
            pltpu.VMEM((TOK, LANES, LANES), bf16),
            pltpu.VMEM((tokens, LANES), bf16),
            pltpu.VMEM((tokens, LANES), bf16),
            pltpu.VMEM((OWNERS, 2, LAGS, LANES), bf16),
            pltpu.VMEM((TOK, LANES, LANES), bf16),
            pltpu.VMEM((OWNERS, LAGS, LANES), bf16),
            pltpu.VMEM((OWNERS, LAGS, LANES), bf16),
            pltpu.VMEM((OWNERS, LAGS, LANES), bf16),
            pltpu.VMEM((OWNERS, LAGS, LANES), bf16),
            spec,
            spec,
            spec,
            pltpu.VMEM((OWNERS, 2, LAGS, LANES), f32),
            dma((4,)),
            dma((TOK,)),
            dma,
            dma((TOK,)),
            dma((TOK,)),
            dma((TOK,)),
            dma((TOK,)),
            dma((OWNERS,)),
            dma((OWNERS,)),
            dma((TOK,)),
            dma((TOK,)),
            dma((OWNERS,)),
            dma((OWNERS,)),
            dma((1 + PAIRS,)),
            dma((1 + PAIRS,)),
            pltpu.SemaphoreType.REGULAR((2,)),
        ],
        compiler_params=pltpu.CompilerParams(
            collective_id=0, has_side_effects=True, vmem_limit_bytes=60 << 20
        ),
        name="gated_conv_backward",
    )(cotangent, gate_values, conv_input, filter_taps.T, ahead, back)
    piece = jax.ShapeDtypeStruct((LAGS, LANES), f32)
    grad_input, new_taps, new_first, new_second = pl.pallas_call(
        update_kernel,
        out_shape=(jax.ShapeDtypeStruct((1, LANES, width), bf16), piece, piece, piece),
        in_specs=[hbm] * 5,
        out_specs=(hbm,) * 4,
        scratch_shapes=[
            pltpu.VMEM((LANES, width), bf16),
            pltpu.VMEM((4, LAGS, LANES), f32),
            pltpu.VMEM((3, LAGS, LANES), f32),
            dma((PIECES,)),
            dma((PIECES,)),
            dma((4,)),
            dma((3,)),
        ],
        compiler_params=pltpu.CompilerParams(vmem_limit_bytes=60 << 20),
        name="filter_update",
    )(blocks, summed, filter_taps.T, first_moment.T, second_moment.T)
    return (grad_input, new_taps.T, new_first.T, new_second.T)


def solution(mesh):
    placed = (
        P("seq", "tok", None),
        P("seq", "tok", None),
        P("seq", "tok", None),
        P("tok", "seq"),
        P("tok", "seq"),
        P("tok", "seq"),
    )
    return jax.shard_map(
        shards,
        mesh=mesh,
        in_specs=placed,
        out_specs=(P("seq", "tok", None), P("tok", "seq"), P("tok", "seq"), P("tok", "seq")),
        check_vma=False,
    )
```
